32 devices in a mesh: grp: 2 (over y), ep: 4 (over z), dp: 4 (over x, core).
Axes of the slice: x: 2, y: 2, z: 4, core: 2. Of those that a mesh axis runs over, the one named last changes fastest.
Arguments:
- hidden_in: bfloat16 [2, 2048, 4096], P(None, ('grp', 'ep', 'dp')), parts along dimension 1, may hold values from -3 to 3
- norm_gain: bfloat16 [4096], replicated, may hold values from 0.099609375 to 1.8984375
- span_plan: int32 [2, 8, 8], P(None, ('grp', 'ep')), parts along dimension 1, may hold values from 0 to 7, each once within a row
- route_ids: int32 [2, 2048, 2], P(None, ('grp', 'ep', 'dp')), parts along dimension 1, may hold values from 0 to 3, all different within a row; in each aligned block of 256 rows (0 to 255, 256 to 511, ..., all dimensions but the last counted through in order) at most 192 rows name the same one
- route_gates: float32 [2, 2048, 2], P(None, ('grp', 'ep', 'dp')), parts along dimension 1, may hold values from 0.1 to 0.6
- w_gate: bfloat16 [4, 4096, 1536], P('ep', 'dp'), may hold values from -0.09375 to 0.09375
- w_up: bfloat16 [4, 4096, 1536], P('ep', 'dp'), may hold values from -0.09375 to 0.09375
- w_down: bfloat16 [4, 1536, 4096], P('ep', None, 'dp'), may hold values from -0.15625 to 0.15625
Outputs:
- mixed: bfloat16 [2, 2048, 4096], P(None, ('grp', 'ep', 'dp')), parts along dimension 1
The draws below stay inside these ranges and needn't reach their ends.
There are 2 independent parts, one for each index of `grp`. The reference program is written for one: setup_inputs(seed, part) draws one part's arguments, and reference() takes and returns one part's arrays. A program takes and returns all parts, laid end to end along the dimension named above; an argument that names none is the same for every part. Nothing has to cross between parts.
Inputs may be any that keep to these rules, and one draw needn't show every extreme that they name: `route_ids`: in each micro-batch, the rows of one ep index (256 rows in a row, aligned) name any expert at most 192 times, a bound that some block reaches; a row names 2 different experts. `span_plan`: for each micro-batch and ep index, a permutation of the 8 spans of that ep index.
All inputs are finite; a program needn't handle non-finite values.
Results may differ from the reference program's by a relative error of at most 0.012.
Values may be sent and summed in bfloat16 or wider, within the bound.
A program may use at most 128 MiB of HBM per device.

```python
import math
import jax
import jax.numpy as jnp
import numpy as np
from jax import lax

D = 4096
FF = 1536
MB = 2
ROUTES = 2
SPANS = 2
TOK_MB = 64
CH = 32
CAP = 192
EXPERTS = 4
TOKENS = 1024
N_EP = 4
N_DP = 4


def steps_of(rng, extent, split, smallest, high):
    loudness = 1.0
    for dim, parts in split:
        heights = jax.random.uniform(jax.random.fold_in(jax.random.fold_in(rng, 6), dim), (parts,), jnp.float32, smallest / len(split), high / len(split))
        loudness = loudness * jnp.repeat(jnp.exp(heights), extent[dim] // parts).reshape((-1,) + (1,) * (len(extent) - 1 - dim))
    return loudness


def deal_out(key, own, number, rows, amount, top, reach, skew):
    ranking = jax.random.permutation(key, amount)
    crowded, common = shares(amount, rows * top, reach, skew, True), shares(amount, rows * top, reach, skew, False)
    places = jnp.arange(amount)

    def named(lengths, rotation):
        used = int((lengths > 0).sum())
        fixed = max(1, used // 4)
        shifted = fixed + (places - fixed + rotation * (used - fixed)) % max(1, amount - fixed)
        return jnp.zeros((amount,), jnp.int32).at[ranking[jnp.where(places < fixed, places, shifted)]].set(jnp.asarray(lengths, jnp.int32))

    lengths = jnp.where(number % 4 == 0, named(crowded, number // 4), named(common, number - number // 4 - 1))
    mixed = jax.random.permutation(jax.random.fold_in(own, 3), amount)
    giver, receiver = mixed[0:amount // 2 * 2:2], mixed[1:amount // 2 * 2:2]
    slack = jnp.minimum(lengths[giver] - 1, reach - lengths[receiver]) // 2
    slack = jnp.where((giver == ranking[0]) | (receiver == ranking[0]) | (lengths[receiver] == 0), 0, jnp.maximum(slack, 0))
    shifted = jax.random.randint(jax.random.fold_in(own, 4), (amount // 2,), 0, 1 << 20) % (slack + 1)
    lengths = lengths.at[giver].add(-shifted).at[receiver].add(shifted)
    members = jnp.searchsorted(jnp.cumsum(lengths), jnp.arange(rows * top), side="right").astype(jnp.int32)
    grid = members.reshape(top, rows).T
    grid = grid[jax.random.permutation(jax.random.fold_in(own, 1), rows)]
    rotation = jax.random.randint(jax.random.fold_in(own, 2), (rows, 1), 0, top)
    return jnp.take_along_axis(grid, (jnp.arange(top)[None, :] + rotation) % top, axis=1)


def shares(amount, total, reach, lean, full):
    weights = [(1 << 20) // math.isqrt(grade ** lean) + 1 for grade in range(1, amount + 1)]
    largest = reach if full else min(reach, max(-(-total // amount), total * weights[0] // sum(weights)))
    least = 1 if total - largest >= amount - 1 else 0
    holding, surplus = [largest] + [least] * (amount - 1), total - largest - least * (amount - 1)
    while surplus > 0:
        free = [i for i in range(1, amount) if holding[i] < largest] or [i for i in range(1, amount) if holding[i] < reach]
        pool, budget = sum([weights[i] for i in free]), surplus
        for i in free:
            addition = min(reach - holding[i], max(1, budget * weights[i] // pool), surplus)
            holding[i] = holding[i] + addition
            surplus = surplus - addition
    return np.array(holding)


def noise(key, extent, spread, most, cuts=(), kind=jnp.bfloat16):
    entries = spread * jax.random.normal(key, extent, jnp.float32)
    if cuts:
        entries = entries * steps_of(key, extent, cuts, -0.22, 0.18)
    return jnp.clip(entries, -most, most).astype(kind)


def setup_inputs(seed: int = 0, part: int = 0) -> dict:
    key_of = jax.random.split(jax.random.key(seed), 9)
    part_keys = jax.random.split(jax.random.fold_in(key_of[8], part), 9)
    hidden_in = noise(part_keys[0], (MB, TOKENS, D), 0.5, 3.0, ((1, 16),))
    norm_gain = jnp.clip(1.0 + 0.18 * jax.random.normal(key_of[1], (D,), jnp.float32), 0.099609375, 1.8984375).astype(jnp.bfloat16)
    span_plan = jax.vmap(lambda own: jax.random.permutation(own, N_DP * SPANS))(jax.random.split(part_keys[2], MB * N_EP)).reshape((MB, N_EP, N_DP * SPANS)).astype(jnp.int32)
    route_ids_keys = jax.random.split(jax.random.fold_in(part_keys[3], 1), MB * TOKENS // (N_DP * TOK_MB))
    route_ids_turns = jax.random.permutation(jax.random.fold_in(part_keys[3], 3), MB * TOKENS // (N_DP * TOK_MB))
    route_ids = jax.vmap(lambda own, number: deal_out(jax.random.fold_in(part_keys[3], 2), own, number, N_DP * TOK_MB, N_EP, ROUTES, CAP, 2))(route_ids_keys, route_ids_turns).reshape((MB, TOKENS, ROUTES))
    route_gates = jnp.clip(jnp.exp(math.log(0.6) - 1.7917595 * jax.random.uniform(part_keys[4], (MB, TOKENS, ROUTES), jnp.float32) ** steps_of(part_keys[4], (MB, TOKENS, ROUTES), ((1, 16),), -0.2, 0.2)), 0.1, 0.6)
    w_gate = noise(key_of[5], (EXPERTS, D, FF), D ** -0.5, 0.09375, ((0, 4), (1, 4)))
    w_up = noise(key_of[6], (EXPERTS, D, FF), D ** -0.5, 0.09375, ((0, 4), (1, 4)))
    w_down = noise(key_of[7], (EXPERTS, FF, D), FF ** -0.5, 0.15625, ((0, 4), (2, 4)))
    return {"hidden_in": hidden_in, "norm_gain": norm_gain, "span_plan": span_plan, "route_ids": route_ids, "route_gates": route_gates, "w_gate": w_gate, "w_up": w_up, "w_down": w_down}


def rms_norm(values, norm_gain):
    wide = values.astype(jnp.float32)
    factor = lax.rsqrt(lax.optimization_barrier(jnp.mean(wide * wide, -1, keepdims=True)) + 1e-06)
    return (wide * factor * norm_gain.astype(jnp.float32)).astype(jnp.bfloat16)

def expert_rows(rows, gate_weight, up_weight, down_weight):
    row_splitter = rows.astype(jnp.float32).reshape(rows.shape[0], N_DP, D // N_DP)

    def sliced_sum(weight):
        block_list = weight.astype(jnp.float32).reshape(N_DP, D // N_DP, FF)
        part_list = jnp.einsum('gep,epv->egv', row_splitter, block_list)
        rounded = lax.optimization_barrier(part_list.astype(jnp.bfloat16))
        return lax.optimization_barrier(jnp.sum(rounded.astype(jnp.float32), 0))
    gate = sliced_sum(gate_weight)
    up_part = sliced_sum(up_weight)
    hidden = (jax.nn.silu(gate) * up_part).astype(jnp.bfloat16)
    return jnp.dot(hidden, down_weight, preferred_element_type=jnp.float32).astype(jnp.bfloat16)

def one_batch(values, plan_rows, route_rows, gate_rows, norm_gain, w_gate, w_up, w_down):
    normed = rms_norm(values, norm_gain)
    flat_ids = route_rows.reshape(-1).astype(jnp.int32)
    route_total = flat_ids.shape[0]
    onehot = (flat_ids[:, None] == jnp.arange(N_EP, dtype=jnp.int32)[None, :]).astype(jnp.int32)
    position = lax.optimization_barrier(jnp.sum((jnp.cumsum(onehot, 0) - 1) * onehot, 1)).astype(jnp.int32)
    depth = N_EP * CAP
    token_of = (jnp.arange(route_total, dtype=jnp.int32) // ROUTES).astype(jnp.int32)
    table = jnp.full((N_EP, depth), TOKENS, jnp.int32).at[flat_ids, position].set(token_of)
    padded = jnp.concatenate([normed, jnp.zeros((1, D), jnp.bfloat16)], 0)

    def run_expert(items):
        return expert_rows(padded[items[0]], items[1], items[2], items[3])
    outputs = lax.map(run_expert, (table, w_gate, w_up, w_down))
    flat_out = outputs.reshape(N_EP * depth, D)
    picked = flat_out[flat_ids * depth + position].astype(jnp.float32).reshape(TOKENS, ROUTES, D)
    moe_sum = lax.optimization_barrier(jnp.sum(picked * gate_rows.astype(jnp.float32)[:, :, None], 1))
    combined = (values.astype(jnp.float32) + moe_sum).astype(jnp.bfloat16)
    block_list = combined.reshape(N_EP, N_DP * SPANS, CH, D)
    moved = jnp.take_along_axis(block_list, plan_rows.astype(jnp.int32)[:, :, None, None], axis=1)
    return moved.reshape(TOKENS, D)

def reference(hidden_in, norm_gain, span_plan, route_ids, route_gates, w_gate, w_up, w_down):
    results = []
    for batch_index in range(MB):
        results.append(one_batch(hidden_in[batch_index], span_plan[batch_index], route_ids[batch_index], route_gates[batch_index], norm_gain, w_gate, w_up, w_down))
    return jnp.stack(results, 0)
```

```python
import jax
import jax.numpy as jnp
from jax import lax
from jax.sharding import PartitionSpec as P

SPANS = 2


def dot32(left, right):
    return jnp.dot(left, right, preferred_element_type=jnp.float32)


def slots_of(ids, ep_count):
    experts = jnp.arange(ep_count, dtype=jnp.float32)
    named = sum((ids[:, r : r + 1] == experts[None, :]).astype(jnp.float32) for r in range(ids.shape[1]))
    rows = ids.shape[0]
    earlier = jnp.arange(rows)[:, None] > jnp.arange(rows)[None, :]
    place = dot32(earlier.astype(jnp.bfloat16), named.astype(jnp.bfloat16))
    return named, place


def local(hidden_in, norm_gain, span_plan, route_ids, route_gates, w_gate, w_up, w_down):
    dp_count = lax.axis_size("dp")
    ep_count = lax.axis_size("ep")
    dp_rank = lax.axis_index("dp")
    batches, tok_rows, width = hidden_in.shape
    routes = route_ids.shape[2]
    span_rows = tok_rows // SPANS
    group_rows = dp_count * tok_rows
    feat = width // dp_count
    hidden_units = w_gate.shape[2]
    capacity = 3 * group_rows * routes // (2 * ep_count)
    slot_count = ep_count * capacity

    split = hidden_in.reshape(batches, tok_rows, dp_count, feat).transpose(2, 0, 1, 3)
    values = lax.all_to_all(split, "dp", split_axis=0, concat_axis=0, tiled=True)
    wide = hidden_in.astype(jnp.float32)
    factor = lax.rsqrt(jnp.mean(wide * wide, -1, keepdims=True) + 1e-06)
    facts = jnp.concatenate([factor, route_ids.astype(jnp.float32), route_gates], -1)
    facts = lax.all_gather(facts, "dp", axis=1, tiled=True)
    gain = lax.dynamic_slice_in_dim(norm_gain, dp_rank * feat, feat, 0).astype(jnp.float32)
    w_both = jnp.concatenate([w_gate[0], w_up[0]], 1)
    w_out = w_down[0]

    experts = jnp.arange(ep_count, dtype=jnp.float32)
    slot_place = jnp.arange(capacity, dtype=jnp.float32)
    rows_in = []
    mixers = []
    received = []
    for m in range(batches):
        rows = values[:, m].reshape(group_rows, feat)
        ids = facts[m, :, 1 : 1 + routes]
        gates = facts[m, :, 1 + routes :]
        normed = (rows.astype(jnp.float32) * facts[m, :, :1] * gain).astype(jnp.bfloat16)
        named, place = slots_of(ids, ep_count)
        where = jnp.where(named > 0, place, -1.0)
        pick = (where.T[:, None, :] == slot_place[None, :, None]).astype(jnp.bfloat16)
        outgoing = dot32(pick.reshape(slot_count, group_rows), normed).astype(jnp.bfloat16)
        received.append(
            lax.all_to_all(
                outgoing.reshape(ep_count, capacity, feat), "ep", split_axis=0, concat_axis=0, tiled=True
            ).reshape(slot_count, feat)
        )
        weight = sum(
            jnp.where(ids[:, r : r + 1] == experts[None, :], gates[:, r : r + 1], 0.0) for r in range(routes)
        )
        plan = span_plan[m, 0]
        table = jnp.concatenate([where, weight], 1).reshape(-1, span_rows, 2 * ep_count)
        table = jnp.take(table, plan, axis=0).reshape(group_rows, 2 * ep_count)
        spread = jnp.where(
            table[:, :ep_count, None] == slot_place[None, None, :], table[:, ep_count:, None], 0.0
        ).reshape(group_rows, slot_count)
        high = spread.astype(jnp.bfloat16)
        low = (spread - high.astype(jnp.float32)).astype(jnp.bfloat16)
        source = (plan[:, None] * span_rows + jnp.arange(span_rows)[None, :]).reshape(-1)
        order = (source[:, None] == jnp.arange(group_rows)[None, :]).astype(jnp.bfloat16)
        mixers.append((high, low, order))
        rows_in.append(rows)

    summed = []
    for m in range(batches):
        parts = dot32(received[m], w_both).astype(jnp.bfloat16)
        summed.append(lax.psum_scatter(parts, "dp", scatter_dimension=0, tiled=True).astype(jnp.float32))
    returned = []
    for m in range(batches):
        hidden = (jax.nn.silu(summed[m][:, :hidden_units]) * summed[m][:, hidden_units:]).astype(jnp.bfloat16)
        hidden = lax.all_gather(hidden, "dp", axis=0, tiled=True)
        expert_out = dot32(hidden, w_out).astype(jnp.bfloat16)
        returned.append(
            lax.all_to_all(
                expert_out.reshape(ep_count, capacity, feat), "ep", split_axis=0, concat_axis=0, tiled=True
            ).reshape(slot_count, feat)
        )
    outputs = []
    for m in range(batches):
        high, low, order = mixers[m]
        total = dot32(high, returned[m]) + dot32(low, returned[m]) + dot32(order, rows_in[m])
        combined = total.astype(jnp.bfloat16).reshape(dp_count, tok_rows, feat)
        outputs.append(lax.all_to_all(combined, "dp", split_axis=0, concat_axis=0, tiled=True))
    return jnp.stack(outputs, 0).transpose(0, 2, 1, 3).reshape(batches, tok_rows, width)


def solution(mesh):
    return jax.shard_map(
        local,
        mesh=mesh,
        in_specs=(
            P(None, ("grp", "ep", "dp"), None),
            P(),
            P(None, ("grp", "ep"), None),
            P(None, ("grp", "ep", "dp"), None),
            P(None, ("grp", "ep", "dp"), None),
            P("ep", "dp", None),
            P("ep", "dp", None),
            P("ep", None, "dp"),
        ),
        out_specs=P(None, ("grp", "ep", "dp"), None),
        check_vma=False,
    )
```

```python
import functools

import jax
import jax.numpy as jnp
from jax import lax
from jax.experimental import pallas as pl
from jax.experimental.pallas import tpu as pltpu
from jax.sharding import PartitionSpec as P

SPANS = 2
UNITS = 4
TILE = 512


def dot32(left, right):
    return jnp.dot(left, right, preferred_element_type=jnp.float32)


def experts_kernel(
    ep_count,
    batches,
    outgoing,
    gate_hbm,
    up_hbm,
    down_hbm,
    returned,
    w_both,
    w_out,
    recv,
    parts,
    pair_in,
    cross_out,
    cross_in,
    hid,
    eo,
    w_sem,
    own_sem,
    z_send,
    z_recv,
    pair_send,
    pair_recv,
    cross_send,
    cross_recv,
    hop_send,
    hop_recv,
    fill_send,
    fill_recv,
    back_send,
    back_recv,
):
    me = lax.axis_index("ep")
    rank = lax.axis_index("dp")
    low, high = lax.rem(rank, 2), rank // 2
    pair = high * 2 + (1 - low)
    cross = (1 - high) * 2 + low
    slots = recv.shape[1]
    capacity = slots // ep_count
    unit = slots // UNITS
    half, quarter = unit // 2, unit // 4
    per_unit = ep_count // UNITS
    units = w_both.shape[1] // 2

    def rows_at(start, size):
        return pl.ds(pl.multiple_of(start, 16), size)

    def remote(src, dst, send, recv_sem, where):
        return pltpu.make_async_remote_copy(
            src_ref=src,
            dst_ref=dst,
            send_sem=send,
            recv_sem=recv_sem,
            device_id=where,
            device_id_type=pl.DeviceIdType.MESH,
        )

    def dispatch(m, s):
        target = lax.rem(me + s, ep_count)
        return remote(
            outgoing.at[m, rows_at(target * capacity, capacity)],
            recv.at[m, pl.ds(s * capacity, capacity)],
            z_send.at[m, s],
            z_recv.at[m, s],
            {"ep": target},
        )

    def give_back(m, s):
        target = lax.rem(me - s + ep_count, ep_count)
        return remote(
            eo.at[m, pl.ds(s * capacity, capacity)],
            returned.at[m, rows_at(me * capacity, capacity)],
            back_send.at[m, s],
            back_recv.at[m, s],
            {"ep": target},
        )

    def own_in(m):
        return pltpu.make_async_copy(
            outgoing.at[m, rows_at(me * capacity, capacity)], recv.at[m, pl.ds(0, capacity)], own_sem.at[m]
        )

    def own_back(m):
        return pltpu.make_async_copy(
            eo.at[m, pl.ds(0, capacity)], returned.at[m, rows_at(me * capacity, capacity)], own_sem.at[batches + m]
        )

    def pair_copy(m, u):
        k = m * UNITS + u
        return remote(
            parts.at[m, rows_at(u * unit + (1 - low) * half, half)],
            pair_in.at[k],
            pair_send.at[k],
            pair_recv.at[k],
            {"dp": pair},
        )

    def cross_copy(m, u):
        k = m * UNITS + u
        return remote(cross_out.at[k], cross_in.at[k], cross_send.at[k], cross_recv.at[k], {"dp": cross})

    def hop_copy(m, u):
        k = m * UNITS + u
        block = hid.at[m, rows_at(u * unit + low * half + high * quarter, quarter)]
        return remote(block, block, hop_send.at[k], hop_recv.at[k], {"dp": cross})

    def fill_copy(m, u):
        k = m * UNITS + u
        block = hid.at[m, rows_at(u * unit + low * half, half)]
        return remote(block, block, fill_send.at[k], fill_recv.at[k], {"dp": pair})

    weights = [
        pltpu.make_async_copy(gate_hbm, w_both.at[:, pl.ds(0, units)], w_sem.at[0]),
        pltpu.make_async_copy(up_hbm, w_both.at[:, pl.ds(units, units)], w_sem.at[1]),
        pltpu.make_async_copy(down_hbm, w_out, w_sem.at[2]),
    ]
    own_in(0).start()
    for copy in weights:
        copy.start()
    for m in range(1, batches):
        own_in(m).start()

    barrier = pltpu.get_barrier_semaphore()
    for s in range(1, ep_count):
        pl.semaphore_signal(
            barrier,
            inc=1,
            device_id={"ep": lax.rem(me + s, ep_count)},
            device_id_type=pl.DeviceIdType.MESH,
        )
    for peer in (pair, cross):
        pl.semaphore_signal(barrier, inc=1, device_id={"dp": peer}, device_id_type=pl.DeviceIdType.MESH)
    pl.semaphore_wait(barrier, ep_count + 1)

    for s in range(1, ep_count):
        dispatch(0, s).start()

    def columns(i):
        return pl.ds(pl.multiple_of(i * TILE, TILE), TILE)

    def project(m, u):
        for s in range(u * per_unit, (u + 1) * per_unit):
            if s == 0:
                own_in(m).wait()
            else:
                dispatch(m, s).wait_recv()
        if m == 0 and u == 0:
            weights[0].wait()
            weights[1].wait()
        rows = pl.ds(u * unit, unit)

        def tile(i, carry):
            parts[m, rows, columns(i)] = dot32(recv[m, rows, :], w_both[:, columns(i)]).astype(jnp.bfloat16)
            return carry

        lax.fori_loop(0, 2 * units // TILE, tile, 0)
        pair_copy(m, u).start()
        if u == 2 and m + 1 < batches:
            for s in range(1, ep_count):
                dispatch(m + 1, s).start()

    def add_pair(m, u):
        k = m * UNITS + u
        pair_copy(m, u).wait_recv()
        mine = rows_at(u * unit + low * half + (1 - high) * quarter, quarter)
        theirs = rows_at((1 - high) * quarter, quarter)

        def tile(i, carry):
            total = parts[m, mine, columns(i)].astype(jnp.float32) + pair_in[k, theirs, columns(i)].astype(jnp.float32)
            cross_out[k, :, columns(i)] = total.astype(jnp.bfloat16)
            return carry

        lax.fori_loop(0, 2 * units // TILE, tile, 0)
        cross_copy(m, u).start()

    def activate(m, u):
        k = m * UNITS + u
        cross_copy(m, u).wait_recv()
        mine = rows_at(u * unit + low * half + high * quarter, quarter)
        theirs = rows_at(high * quarter, quarter)

        def total(cols):
            return (
                parts[m, mine, cols].astype(jnp.float32)
                + pair_in[k, theirs, cols].astype(jnp.float32)
                + cross_in[k, :, cols].astype(jnp.float32)
            )

        def tile(i, carry):
            gate = total(columns(i))
            up = total(pl.ds(pl.multiple_of(units + i * TILE, TILE), TILE))
            hid[m, mine, columns(i)] = (jax.nn.silu(gate) * up).astype(jnp.bfloat16)
            return carry

        lax.fori_loop(0, units // TILE, tile, 0)
        hop_copy(m, u).start()

    def forward(m, u):
        hop_copy(m, u).wait_recv()
        fill_copy(m, u).start()

    def finish(m, u):
        fill_copy(m, u).wait_recv()
        if m == 0 and u == 0:
            weights[2].wait()
        rows = pl.ds(u * unit, unit)

        def tile(i, carry):
            eo[m, rows, columns(i)] = dot32(hid[m, rows, :], w_out[:, columns(i)]).astype(jnp.bfloat16)
            return carry

        lax.fori_loop(0, w_out.shape[1] // TILE, tile, 0)
        for s in range(u * per_unit, (u + 1) * per_unit):
            if s == 0:
                own_back(m).start()
            else:
                give_back(m, s).start()

    steps = [(m, u) for m in range(batches) for u in range(UNITS)]
    stages = (project, add_pair, activate, forward, finish)
    for step in range(len(steps) + len(stages) - 1):
        for lag, stage in enumerate(stages):
            if 0 <= step - lag < len(steps):
                stage(*steps[step - lag])

    for m, u in steps:
        pair_copy(m, u).wait_send()
        cross_copy(m, u).wait_send()
        hop_copy(m, u).wait_send()
        fill_copy(m, u).wait_send()
    for m in range(batches):
        own_back(m).wait()
        for s in range(1, ep_count):
            dispatch(m, s).wait_send()
            give_back(m, s).wait_send()
            back_from = lax.rem(me + s, ep_count)
            remote(
                eo.at[m, pl.ds(s * capacity, capacity)],
                returned.at[m, rows_at(back_from * capacity, capacity)],
                back_send.at[m, s],
                back_recv.at[m, s],
                {"ep": back_from},
            ).wait_recv()


def run_experts(outgoing, gate, up, down, ep_count):
    batches, slots, feat = outgoing.shape
    units = gate.shape[1]
    count = batches * UNITS
    unit = slots // UNITS
    half, quarter = unit // 2, unit // 4
    bf16 = jnp.bfloat16
    dma = pltpu.SemaphoreType.DMA
    return pl.pallas_call(
        functools.partial(experts_kernel, ep_count, batches),
        out_shape=jax.ShapeDtypeStruct((batches, slots, feat), bf16),
        in_specs=[pl.BlockSpec(memory_space=pl.ANY)] * 4,
        out_specs=pl.BlockSpec(memory_space=pl.ANY),
        scratch_shapes=[
            pltpu.VMEM((feat, 2 * units), bf16),
            pltpu.VMEM((units, feat), bf16),
            pltpu.VMEM((batches, slots, feat), bf16),
            pltpu.VMEM((batches, slots, 2 * units), bf16),
            pltpu.VMEM((count, half, 2 * units), bf16),
            pltpu.VMEM((count, quarter, 2 * units), bf16),
            pltpu.VMEM((count, quarter, 2 * units), bf16),
            pltpu.VMEM((batches, slots, units), bf16),
            pltpu.VMEM((batches, slots, feat), bf16),
            dma((3,)),
            dma((2 * batches,)),
            dma((batches, ep_count)),
            dma((batches, ep_count)),
            dma((count,)),
            dma((count,)),
            dma((count,)),
            dma((count,)),
            dma((count,)),
            dma((count,)),
            dma((count,)),
            dma((count,)),
            dma((batches, ep_count)),
            dma((batches, ep_count)),
        ],
        compiler_params=pltpu.CompilerParams(
            collective_id=0, has_side_effects=True, vmem_limit_bytes=60 * 1024 * 1024
        ),
        cost_estimate=pl.CostEstimate(
            flops=6 * batches * slots * feat * units, bytes_accessed=20 * 2**20, transcendentals=batches * slots * units
        ),
    )(outgoing, gate, up, down)


def local(hidden_in, norm_gain, span_plan, route_ids, route_gates, w_gate, w_up, w_down):
    dp_count = lax.axis_size("dp")
    ep_count = lax.axis_size("ep")
    dp_rank = lax.axis_index("dp")
    batches, tok_rows, width = hidden_in.shape
    routes = route_ids.shape[2]
    span_rows = tok_rows // SPANS
    group_rows = dp_count * tok_rows
    feat = width // dp_count
    capacity = -(-3 * group_rows * routes // (2 * ep_count) // 16) * 16
    slot_count = ep_count * capacity

    split = hidden_in.reshape(batches, tok_rows, dp_count, feat).transpose(2, 0, 1, 3)
    values = lax.all_to_all(split, "dp", split_axis=0, concat_axis=0, tiled=True)
    rows = values.transpose(1, 0, 2, 3).reshape(batches, group_rows, feat)
    wide = hidden_in.astype(jnp.float32)
    factor = lax.rsqrt(jnp.mean(wide * wide, -1, keepdims=True) + 1e-06)
    facts = jnp.concatenate([factor, route_ids.astype(jnp.float32), route_gates], -1)
    facts = lax.all_gather(facts, "dp", axis=1, tiled=True)
    ids = facts[:, :, 1 : 1 + routes, None]
    gates = facts[:, :, 1 + routes :, None]
    gain = lax.dynamic_slice_in_dim(norm_gain, dp_rank * feat, feat, 0).astype(jnp.float32)

    experts = jnp.arange(ep_count, dtype=jnp.float32)
    slot_place = jnp.arange(capacity, dtype=jnp.float32)
    chosen = ids == experts
    named = jnp.sum(chosen.astype(jnp.float32), 2)
    weight = jnp.sum(jnp.where(chosen, gates, 0.0), 2)
    numbers = jnp.arange(group_rows)
    earlier = (numbers[:, None] > numbers[None, :]).astype(jnp.bfloat16)
    place = jnp.einsum("ts,mse->mte", earlier, named.astype(jnp.bfloat16), preferred_element_type=jnp.float32)
    where = jnp.where(named > 0, place, -1.0)
    pick = (where.transpose(0, 2, 1)[:, :, None, :] == slot_place[None, None, :, None]).astype(jnp.bfloat16)
    pick = pick.reshape(batches, slot_count, group_rows)
    normed = (rows.astype(jnp.float32) * facts[:, :, :1] * gain).astype(jnp.bfloat16)
    outgoing = jnp.einsum("mst,mtf->msf", pick, normed, preferred_element_type=jnp.float32).astype(jnp.bfloat16)

    plan = span_plan[:, 0]
    table = jnp.concatenate([where, weight], 2).reshape(batches, -1, span_rows, 2 * ep_count)
    table = jnp.take_along_axis(table, plan[:, :, None, None], axis=1).reshape(batches, group_rows, 2 * ep_count)
    spread = jnp.where(
        table[:, :, :ep_count, None] == slot_place, table[:, :, ep_count:, None], 0.0
    ).reshape(batches, group_rows, slot_count)
    high = spread.astype(jnp.bfloat16)
    low = (spread - high.astype(jnp.float32)).astype(jnp.bfloat16)
    source = (plan[:, :, None] * span_rows + jnp.arange(span_rows)).reshape(batches, group_rows)
    order = (source[:, :, None] == numbers).astype(jnp.bfloat16)

    returned = run_experts(outgoing, w_gate[0], w_up[0], w_down[0], ep_count)

    def mix(left, right):
        return jnp.einsum("mts,msf->mtf", left, right, preferred_element_type=jnp.float32)

    total = mix(high, returned) + mix(low, returned) + mix(order, rows)
    combined = total.astype(jnp.bfloat16).reshape(batches, dp_count, tok_rows, feat).transpose(1, 0, 2, 3)
    outputs = lax.all_to_all(combined, "dp", split_axis=0, concat_axis=0, tiled=True)
    return outputs.transpose(1, 2, 0, 3).reshape(batches, tok_rows, width)


def solution(mesh):
    return jax.shard_map(
        local,
        mesh=mesh,
        in_specs=(
            P(None, ("grp", "ep", "dp"), None),
            P(),
            P(None, ("grp", "ep"), None),
            P(None, ("grp", "ep", "dp"), None),
            P(None, ("grp", "ep", "dp"), None),
            P("ep", "dp", None),
            P("ep", "dp", None),
            P("ep", None, "dp"),
        ),
        out_specs=P(None, ("grp", "ep", "dp"), None),
        check_vma=False,
    )
```

```python
import functools

import jax
import jax.numpy as jnp
from jax import lax
from jax.experimental import pallas as pl
from jax.experimental.pallas import tpu as pltpu
from jax.sharding import PartitionSpec as P

SPANS = 2
UNITS = 4
TILE = 512


def dot32(left, right):
    return jnp.dot(left, right, preferred_element_type=jnp.float32)


def experts_kernel(
    ep_count,
    batches,
    tokens,
    pick,
    factor,
    gain,
    mix_high,
    mix_low,
    order,
    gate_hbm,
    up_hbm,
    down_hbm,
    mixed,
    w_both,
    w_out,
    rows_in,
    outgoing,
    returned,
    recv,
    parts,
    pair_in,
    cross_in,
    hid,
    eo,
    w_sem,
    own_sem,
    z_send,
    z_recv,
    pair_send,
    pair_recv,
    cross_send,
    cross_recv,
    hop_send,
    hop_recv,
    fill_send,
    fill_recv,
    back_send,
    back_recv,
    in_send,
    in_recv,
    out_send,
    out_recv,
    edge_sem,
):
    me = lax.axis_index("ep")
    rank = lax.axis_index("dp")
    low, high = lax.rem(rank, 2), rank // 2
    pair = high * 2 + (1 - low)
    cross = (1 - high) * 2 + low
    slots = recv.shape[1]
    capacity = slots // ep_count
    unit = slots // UNITS
    half, quarter = unit // 2, unit // 4
    per_unit = ep_count // UNITS
    units = w_both.shape[1] // 2
    tok_rows = tokens.shape[1]
    feat = rows_in.shape[2]
    across = (1 - high) * 2 + (1 - low)
    peers = (across, cross, pair)

    def rows_at(start, size):
        return pl.ds(pl.multiple_of(start, 16), size)

    def remote(src, dst, send, recv_sem, where):
        return pltpu.make_async_remote_copy(
            src_ref=src,
            dst_ref=dst,
            send_sem=send,
            recv_sem=recv_sem,
            device_id=where,
            device_id_type=pl.DeviceIdType.MESH,
        )

    def dispatch(m, s):
        target = lax.rem(me + s, ep_count)
        return remote(
            outgoing.at[m, rows_at(target * capacity, capacity)],
            recv.at[m, pl.ds(s * capacity, capacity)],
            z_send.at[m, s],
            z_recv.at[m, s],
            {"ep": target},
        )

    def give_back(m, s):
        target = lax.rem(me - s + ep_count, ep_count)
        return remote(
            eo.at[m, pl.ds(s * capacity, capacity)],
            returned.at[m, rows_at(me * capacity, capacity)],
            back_send.at[m, s],
            back_recv.at[m, s],
            {"ep": target},
        )

    def feats_at(owner):
        return pl.ds(pl.multiple_of(owner * feat, 128), feat)

    def slice_out(m, p):
        return remote(
            tokens.at[m, :, feats_at(peers[p])],
            rows_in.at[m, rows_at(rank * tok_rows, tok_rows)],
            in_send.at[m, p],
            in_recv.at[m, p],
            {"dp": peers[p]},
        )

    def own_slice(m):
        return pltpu.make_async_copy(
            tokens.at[m, :, feats_at(rank)], rows_in.at[m, rows_at(rank * tok_rows, tok_rows)], edge_sem.at[m]
        )

    def row_back(m, p):
        return remote(
            rows_in.at[m, rows_at(peers[p] * tok_rows, tok_rows)],
            mixed.at[m, :, feats_at(rank)],
            out_send.at[m, p],
            out_recv.at[m, p],
            {"dp": peers[p]},
        )

    def own_row_back(m):
        return pltpu.make_async_copy(
            rows_in.at[m, rows_at(rank * tok_rows, tok_rows)],
            mixed.at[m, :, feats_at(rank)],
            edge_sem.at[batches + m],
        )

    def own_in(m):
        return pltpu.make_async_copy(
            outgoing.at[m, rows_at(me * capacity, capacity)], recv.at[m, pl.ds(0, capacity)], own_sem.at[m]
        )

    def own_back(m):
        return pltpu.make_async_copy(
            eo.at[m, pl.ds(0, capacity)], returned.at[m, rows_at(me * capacity, capacity)], own_sem.at[batches + m]
        )

    def pair_copy(m, u):
        k = m * UNITS + u
        return remote(
            parts.at[m, rows_at(u * unit + (1 - low) * half, half)],
            pair_in.at[k],
            pair_send.at[k],
            pair_recv.at[k],
            {"dp": pair},
        )

    def cross_copy(m, u):
        k = m * UNITS + u
        return remote(pair_in.at[k, rows_at((1 - high) * quarter, quarter)], cross_in.at[k], cross_send.at[k], cross_recv.at[k], {"dp": cross})

    def hop_copy(m, u):
        k = m * UNITS + u
        block = hid.at[m, rows_at(u * unit + low * half + high * quarter, quarter)]
        return remote(block, block, hop_send.at[k], hop_recv.at[k], {"dp": cross})

    def fill_copy(m, u):
        k = m * UNITS + u
        block = hid.at[m, rows_at(u * unit + low * half, half)]
        return remote(block, block, fill_send.at[k], fill_recv.at[k], {"dp": pair})

    weights = [
        pltpu.make_async_copy(gate_hbm, w_both.at[:, pl.ds(0, units)], w_sem.at[0]),
        pltpu.make_async_copy(up_hbm, w_both.at[:, pl.ds(units, units)], w_sem.at[1]),
        pltpu.make_async_copy(down_hbm, w_out, w_sem.at[2]),
    ]
    for m in range(batches):
        own_slice(m).start()

    barrier = pltpu.get_barrier_semaphore()
    for s in range(1, ep_count):
        pl.semaphore_signal(
            barrier,
            inc=1,
            device_id={"ep": lax.rem(me + s, ep_count)},
            device_id_type=pl.DeviceIdType.MESH,
        )
    for peer in peers:
        pl.semaphore_signal(barrier, inc=1, device_id={"dp": peer}, device_id_type=pl.DeviceIdType.MESH)
    pl.semaphore_wait(barrier, ep_count + 2)

    for m in range(batches):
        for p in range(len(peers)):
            slice_out(m, p).start()
    for copy in weights:
        copy.start()

    def columns(i):
        return pl.ds(pl.multiple_of(i * TILE, TILE), TILE)

    def prepare(m):
        own_slice(m).wait()
        for p in range(len(peers)):
            slice_out(m, p).wait_recv()

        def tile(i, carry):
            wide = rows_in[m, :, columns(i)].astype(jnp.float32)
            normed = (wide * factor[m] * gain[:, columns(i)]).astype(jnp.bfloat16)
            outgoing[m, :, columns(i)] = dot32(pick[m], normed).astype(jnp.bfloat16)
            return carry

        lax.fori_loop(0, feat // TILE, tile, 0)
        own_in(m).start()

    def combine(m):
        own_back(m).wait()
        for s in range(1, ep_count):
            back_from = lax.rem(me + s, ep_count)
            remote(
                eo.at[m, pl.ds(s * capacity, capacity)],
                returned.at[m, rows_at(back_from * capacity, capacity)],
                back_send.at[m, s],
                back_recv.at[m, s],
                {"ep": back_from},
            ).wait_recv()

        def tile(i, carry):
            back = returned[m, :, columns(i)]
            total = dot32(mix_high[m], back) + dot32(mix_low[m], back) + dot32(order[m], rows_in[m, :, columns(i)])
            rows_in[m, :, columns(i)] = total.astype(jnp.bfloat16)
            return carry

        lax.fori_loop(0, feat // TILE, tile, 0)
        for p in range(len(peers)):
            row_back(m, p).start()
        own_row_back(m).start()

    prepare(0)
    for s in range(1, ep_count):
        dispatch(0, s).start()
    for m in range(1, batches):
        prepare(m)

    def project(m, u):
        for s in range(u * per_unit, (u + 1) * per_unit):
            if s == 0:
                own_in(m).wait()
            else:
                dispatch(m, s).wait_recv()
        if m == 0 and u == 0:
            weights[0].wait()
            weights[1].wait()
        rows = pl.ds(u * unit, unit)

        def tile(i, carry):
            parts[m, rows, columns(i)] = dot32(recv[m, rows, :], w_both[:, columns(i)]).astype(jnp.bfloat16)
            return carry

        lax.fori_loop(0, 2 * units // TILE, tile, 0)
        pair_copy(m, u).start()
        if u == 2 and m + 1 < batches:
            for s in range(1, ep_count):
                dispatch(m + 1, s).start()

    def add_pair(m, u):
        k = m * UNITS + u
        pair_copy(m, u).wait_recv()
        mine = rows_at(u * unit + low * half + (1 - high) * quarter, quarter)
        theirs = rows_at((1 - high) * quarter, quarter)

        def tile(i, carry):
            total = parts[m, mine, columns(i)].astype(jnp.float32) + pair_in[k, theirs, columns(i)].astype(jnp.float32)
            pair_in[k, theirs, columns(i)] = total.astype(jnp.bfloat16)
            return carry

        lax.fori_loop(0, 2 * units // TILE, tile, 0)
        cross_copy(m, u).start()

    def activate(m, u):
        k = m * UNITS + u
        cross_copy(m, u).wait_recv()
        mine = rows_at(u * unit + low * half + high * quarter, quarter)
        theirs = rows_at(high * quarter, quarter)

        def total(cols):
            return (
                parts[m, mine, cols].astype(jnp.float32)
                + pair_in[k, theirs, cols].astype(jnp.float32)
                + cross_in[k, :, cols].astype(jnp.float32)
            )

        def tile(i, carry):
            gate = total(columns(i))
            up = total(pl.ds(pl.multiple_of(units + i * TILE, TILE), TILE))
            hid[m, mine, columns(i)] = (jax.nn.silu(gate) * up).astype(jnp.bfloat16)
            return carry

        lax.fori_loop(0, units // TILE, tile, 0)
        hop_copy(m, u).start()

    def forward(m, u):
        hop_copy(m, u).wait_recv()
        fill_copy(m, u).start()

    def finish(m, u):
        fill_copy(m, u).wait_recv()
        if m == 0 and u == 0:
            weights[2].wait()
        rows = pl.ds(u * unit, unit)

        def tile(i, carry):
            eo[m, rows, columns(i)] = dot32(hid[m, rows, :], w_out[:, columns(i)]).astype(jnp.bfloat16)
            return carry

        lax.fori_loop(0, w_out.shape[1] // TILE, tile, 0)
        for s in range(u * per_unit, (u + 1) * per_unit):
            if s == 0:
                own_back(m).start()
            else:
                give_back(m, s).start()

    steps = [(m, u) for m in range(batches) for u in range(UNITS)]
    stages = (project, add_pair, activate, forward, finish)
    for step in range(len(steps) + len(stages) - 1):
        for lag, stage in enumerate(stages):
            if 0 <= step - lag < len(steps):
                stage(*steps[step - lag])

    for m in range(batches):
        combine(m)
    for m, u in steps:
        pair_copy(m, u).wait_send()
        cross_copy(m, u).wait_send()
        hop_copy(m, u).wait_send()
        fill_copy(m, u).wait_send()
    for m in range(batches):
        for s in range(1, ep_count):
            dispatch(m, s).wait_send()
            give_back(m, s).wait_send()
        own_row_back(m).wait()
        for p in range(len(peers)):
            slice_out(m, p).wait_send()
            row_back(m, p).wait_send()
            remote(
                rows_in.at[m, rows_at(peers[p] * tok_rows, tok_rows)],
                mixed.at[m, :, feats_at(peers[p])],
                out_send.at[m, p],
                out_recv.at[m, p],
                {"dp": peers[p]},
            ).wait_recv()


def run_experts(tokens, pick, factor, gain, mixers, gate, up, down, ep_count):
    batches, slots, group_rows = pick.shape
    feat = down.shape[1]
    units = gate.shape[1]
    count = batches * UNITS
    unit = slots // UNITS
    half, quarter = unit // 2, unit // 4
    bf16 = jnp.bfloat16
    dma = pltpu.SemaphoreType.DMA
    return pl.pallas_call(
        functools.partial(experts_kernel, ep_count, batches),
        out_shape=jax.ShapeDtypeStruct(tokens.shape, bf16),
        in_specs=[pl.BlockSpec(memory_space=pl.ANY)]
        + [pl.BlockSpec(memory_space=pltpu.VMEM)] * 6
        + [pl.BlockSpec(memory_space=pl.ANY)] * 3,
        out_specs=pl.BlockSpec(memory_space=pl.ANY),
        scratch_shapes=[
            pltpu.VMEM((feat, 2 * units), bf16),
            pltpu.VMEM((units, feat), bf16),
            pltpu.VMEM((batches, group_rows, feat), bf16),
            pltpu.VMEM((batches, slots, feat), bf16),
            pltpu.VMEM((batches, slots, feat), bf16),
            pltpu.VMEM((batches, slots, feat), bf16),
            pltpu.VMEM((batches, slots, 2 * units), bf16),
            pltpu.VMEM((count, half, 2 * units), bf16),
            pltpu.VMEM((count, quarter, 2 * units), bf16),
            pltpu.VMEM((batches, slots, units), bf16),
            pltpu.VMEM((batches, slots, feat), bf16),
            dma((3,)),
            dma((2 * batches,)),
            dma((batches, ep_count)),
            dma((batches, ep_count)),
            dma((count,)),
            dma((count,)),
            dma((count,)),
            dma((count,)),
            dma((count,)),
            dma((count,)),
            dma((count,)),
            dma((count,)),
            dma((batches, ep_count)),
            dma((batches, ep_count)),
            dma((batches, 3)),
            dma((batches, 3)),
            dma((batches, 3)),
            dma((batches, 3)),
            dma((2 * batches,)),
        ],
        compiler_params=pltpu.CompilerParams(
            collective_id=0, has_side_effects=True, vmem_limit_bytes=60 * 1024 * 1024
        ),
        cost_estimate=pl.CostEstimate(
            flops=6 * batches * slots * feat * units, bytes_accessed=20 * 2**20, transcendentals=batches * slots * units
        ),
    )(tokens, pick, factor, gain, *mixers, gate, up, down)


def local(hidden_in, norm_gain, span_plan, route_ids, route_gates, w_gate, w_up, w_down):
    dp_count = lax.axis_size("dp")
    ep_count = lax.axis_size("ep")
    dp_rank = lax.axis_index("dp")
    batches, tok_rows, width = hidden_in.shape
    routes = route_ids.shape[2]
    span_rows = tok_rows // SPANS
    group_rows = dp_count * tok_rows
    feat = width // dp_count
    capacity = -(-3 * group_rows * routes // (2 * ep_count) // 16) * 16
    slot_count = ep_count * capacity

    wide = hidden_in.astype(jnp.float32)
    factor = lax.rsqrt(jnp.mean(wide * wide, -1, keepdims=True) + 1e-06)
    facts = jnp.concatenate([factor, route_ids.astype(jnp.float32), route_gates], -1)
    facts = lax.all_gather(facts, "dp", axis=1, tiled=True)
    ids = facts[:, :, 1 : 1 + routes, None]
    gates = facts[:, :, 1 + routes :, None]
    gain = lax.dynamic_slice_in_dim(norm_gain, dp_rank * feat, feat, 0).astype(jnp.float32)

    experts = jnp.arange(ep_count, dtype=jnp.float32)
    slot_place = jnp.arange(capacity, dtype=jnp.float32)
    chosen = ids == experts
    named = jnp.sum(chosen.astype(jnp.float32), 2)
    weight = jnp.sum(jnp.where(chosen, gates, 0.0), 2)
    numbers = jnp.arange(group_rows)
    earlier = (numbers[:, None] > numbers[None, :]).astype(jnp.bfloat16)
    place = jnp.einsum("ts,mse->mte", earlier, named.astype(jnp.bfloat16), preferred_element_type=jnp.float32)
    where = jnp.where(named > 0, place, -1.0)
    pick = (where.transpose(0, 2, 1)[:, :, None, :] == slot_place[None, None, :, None]).astype(jnp.bfloat16)
    pick = pick.reshape(batches, slot_count, group_rows)
    plan = span_plan[:, 0]
    table = jnp.concatenate([where, weight], 2).reshape(batches, -1, span_rows, 2 * ep_count)
    table = jnp.take_along_axis(table, plan[:, :, None, None], axis=1).reshape(batches, group_rows, 2 * ep_count)
    spread = jnp.where(
        table[:, :, :ep_count, None] == slot_place, table[:, :, ep_count:, None], 0.0
    ).reshape(batches, group_rows, slot_count)
    high = spread.astype(jnp.bfloat16)
    low = (spread - high.astype(jnp.float32)).astype(jnp.bfloat16)
    source = (plan[:, :, None] * span_rows + jnp.arange(span_rows)).reshape(batches, group_rows)
    order = (source[:, :, None] == numbers).astype(jnp.bfloat16)

    return run_experts(
        hidden_in,
        pick,
        facts[:, :, :1],
        gain[None, :],
        (high, low, order),
        w_gate[0],
        w_up[0],
        w_down[0],
        ep_count,
    )


def solution(mesh):
    return jax.shard_map(
        local,
        mesh=mesh,
        in_specs=(
            P(None, ("grp", "ep", "dp"), None),
            P(),
            P(None, ("grp", "ep"), None),
            P(None, ("grp", "ep", "dp"), None),
            P(None, ("grp", "ep", "dp"), None),
            P("ep", "dp", None),
            P("ep", "dp", None),
            P("ep", None, "dp"),
        ),
        out_specs=P(None, ("grp", "ep", "dp"), None),
        check_vma=False,
    )
```

```python
import functools

import jax
import jax.numpy as jnp
from jax import lax
from jax.experimental import pallas as pl
from jax.experimental.pallas import tpu as pltpu
from jax.sharding import PartitionSpec as P

SPANS = 2
UNITS = 4
TILE = 512


def dot32(left, right):
    return jnp.dot(left, right, preferred_element_type=jnp.float32)


def experts_kernel(
    ep_count,
    batches,
    tokens,
    pick,
    factor,
    gain,
    table,
    gate_hbm,
    up_hbm,
    down_hbm,
    mixed,
    w_both,
    w_out,
    rows_in,
    outgoing,
    returned,
    mix_high,
    mix_low,
    order,
    recv,
    parts,
    pair_in,
    cross_in,
    hid,
    eo,
    w_sem,
    own_sem,
    z_send,
    z_recv,
    pair_send,
    pair_recv,
    cross_send,
    cross_recv,
    hop_send,
    hop_recv,
    fill_send,
    fill_recv,
    back_send,
    back_recv,
    in_send,
    in_recv,
    out_send,
    out_recv,
    edge_sem,
):
    me = lax.axis_index("ep")
    rank = lax.axis_index("dp")
    low, high = lax.rem(rank, 2), rank // 2
    pair = high * 2 + (1 - low)
    cross = (1 - high) * 2 + low
    slots = recv.shape[1]
    capacity = slots // ep_count
    unit = slots // UNITS
    half, quarter = unit // 2, unit // 4
    per_unit = ep_count // UNITS
    units = w_both.shape[1] // 2
    tok_rows = tokens.shape[1]
    feat = rows_in.shape[2]
    across = (1 - high) * 2 + (1 - low)
    peers = (across, cross, pair)

    def rows_at(start, size):
        return pl.ds(pl.multiple_of(start, 16), size)

    def remote(src, dst, send, recv_sem, where):
        return pltpu.make_async_remote_copy(
            src_ref=src,
            dst_ref=dst,
            send_sem=send,
            recv_sem=recv_sem,
            device_id=where,
            device_id_type=pl.DeviceIdType.MESH,
        )

    def dispatch(m, s):
        target = lax.rem(me + s, ep_count)
        return remote(
            outgoing.at[m, rows_at(target * capacity, capacity)],
            recv.at[m, pl.ds(s * capacity, capacity)],
            z_send.at[m, s],
            z_recv.at[m, s],
            {"ep": target},
        )

    def give_back(m, s):
        target = lax.rem(me - s + ep_count, ep_count)
        return remote(
            eo.at[m, pl.ds(s * capacity, capacity)],
            returned.at[m, rows_at(me * capacity, capacity)],
            back_send.at[m, s],
            back_recv.at[m, s],
            {"ep": target},
        )

    def feats_at(owner):
        return pl.ds(pl.multiple_of(owner * feat, 128), feat)

    def slice_out(m, p):
        return remote(
            tokens.at[m, :, feats_at(peers[p])],
            rows_in.at[m, rows_at(rank * tok_rows, tok_rows)],
            in_send.at[m, p],
            in_recv.at[m, p],
            {"dp": peers[p]},
        )

    def own_slice(m):
        return pltpu.make_async_copy(
            tokens.at[m, :, feats_at(rank)], rows_in.at[m, rows_at(rank * tok_rows, tok_rows)], edge_sem.at[m]
        )

    def row_back(m, p):
        return remote(
            rows_in.at[m, rows_at(peers[p] * tok_rows, tok_rows)],
            mixed.at[m, :, feats_at(rank)],
            out_send.at[m, p],
            out_recv.at[m, p],
            {"dp": peers[p]},
        )

    def own_row_back(m):
        return pltpu.make_async_copy(
            rows_in.at[m, rows_at(rank * tok_rows, tok_rows)],
            mixed.at[m, :, feats_at(rank)],
            edge_sem.at[batches + m],
        )

    def own_in(m):
        return pltpu.make_async_copy(
            outgoing.at[m, rows_at(me * capacity, capacity)], recv.at[m, pl.ds(0, capacity)], own_sem.at[m]
        )

    def own_back(m):
        return pltpu.make_async_copy(
            eo.at[m, pl.ds(0, capacity)], returned.at[m, rows_at(me * capacity, capacity)], own_sem.at[batches + m]
        )

    def pair_copy(m, u):
        k = m * UNITS + u
        return remote(
            parts.at[m, rows_at(u * unit + (1 - low) * half, half)],
            pair_in.at[k],
            pair_send.at[k],
            pair_recv.at[k],
            {"dp": pair},
        )

    def cross_copy(m, u):
        k = m * UNITS + u
        return remote(pair_in.at[k, rows_at((1 - high) * quarter, quarter)], cross_in.at[k], cross_send.at[k], cross_recv.at[k], {"dp": cross})

    def hop_copy(m, u):
        k = m * UNITS + u
        block = hid.at[m, rows_at(u * unit + low * half + high * quarter, quarter)]
        return remote(block, block, hop_send.at[k], hop_recv.at[k], {"dp": cross})

    def fill_copy(m, u):
        k = m * UNITS + u
        block = hid.at[m, rows_at(u * unit + low * half, half)]
        return remote(block, block, fill_send.at[k], fill_recv.at[k], {"dp": pair})

    weights = [
        pltpu.make_async_copy(gate_hbm, w_both.at[:, pl.ds(0, units)], w_sem.at[0]),
        pltpu.make_async_copy(up_hbm, w_both.at[:, pl.ds(units, units)], w_sem.at[1]),
        pltpu.make_async_copy(down_hbm, w_out, w_sem.at[2]),
    ]
    for m in range(batches):
        own_slice(m).start()

    barrier = pltpu.get_barrier_semaphore()
    for s in range(1, ep_count):
        pl.semaphore_signal(
            barrier,
            inc=1,
            device_id={"ep": lax.rem(me + s, ep_count)},
            device_id_type=pl.DeviceIdType.MESH,
        )
    for peer in peers:
        pl.semaphore_signal(barrier, inc=1, device_id={"dp": peer}, device_id_type=pl.DeviceIdType.MESH)
    pl.semaphore_wait(barrier, ep_count + 2)

    for m in range(batches):
        for p in range(len(peers)):
            slice_out(m, p).start()
    for copy in weights:
        copy.start()

    def columns(i):
        return pl.ds(pl.multiple_of(i * TILE, TILE), TILE)

    def prepare(m):
        own_slice(m).wait()
        for p in range(len(peers)):
            slice_out(m, p).wait_recv()

        def tile(i, carry):
            wide = rows_in[m, :, columns(i)].astype(jnp.float32)
            normed = (wide * factor[m] * gain[:, columns(i)]).astype(jnp.bfloat16)
            outgoing[m, :, columns(i)] = dot32(pick[m], normed).astype(jnp.bfloat16)
            return carry

        lax.fori_loop(0, feat // TILE, tile, 0)
        own_in(m).start()

    def weigh(m):
        group_rows = table.shape[1]
        routes = (table.shape[2] - 1) // 2
        number = lax.broadcasted_iota(jnp.int32, (group_rows, slots), 1).astype(jnp.float32)
        spread = jnp.zeros((group_rows, slots), jnp.float32)
        for r in range(routes):
            spread += jnp.where(table[m, :, r : r + 1] == number, table[m, :, routes + r : routes + r + 1], 0.0)
        top = spread.astype(jnp.bfloat16)
        mix_high[m] = top
        mix_low[m] = (spread - top.astype(jnp.float32)).astype(jnp.bfloat16)
        source = lax.broadcasted_iota(jnp.int32, (group_rows, group_rows), 1).astype(jnp.float32)
        order[m] = jnp.where(table[m, :, 2 * routes :] == source, 1.0, 0.0).astype(jnp.bfloat16)

    def combine(m):
        own_back(m).wait()
        for s in range(1, ep_count):
            back_from = lax.rem(me + s, ep_count)
            remote(
                eo.at[m, pl.ds(s * capacity, capacity)],
                returned.at[m, rows_at(back_from * capacity, capacity)],
                back_send.at[m, s],
                back_recv.at[m, s],
                {"ep": back_from},
            ).wait_recv()

        def tile(i, carry):
            back = returned[m, :, columns(i)]
            total = dot32(mix_high[m], back) + dot32(mix_low[m], back) + dot32(order[m], rows_in[m, :, columns(i)])
            rows_in[m, :, columns(i)] = total.astype(jnp.bfloat16)
            return carry

        lax.fori_loop(0, feat // TILE, tile, 0)
        for p in range(len(peers)):
            row_back(m, p).start()
        own_row_back(m).start()

    prepare(0)
    for s in range(1, ep_count):
        dispatch(0, s).start()
    for m in range(1, batches):
        prepare(m)
    for m in range(batches):
        weigh(m)

    def project(m, u):
        for s in range(u * per_unit, (u + 1) * per_unit):
            if s == 0:
                own_in(m).wait()
            else:
                dispatch(m, s).wait_recv()
        if m == 0 and u == 0:
            weights[0].wait()
            weights[1].wait()
        rows = pl.ds(u * unit, unit)

        def tile(i, carry):
            parts[m, rows, columns(i)] = dot32(recv[m, rows, :], w_both[:, columns(i)]).astype(jnp.bfloat16)
            return carry

        lax.fori_loop(0, 2 * units // TILE, tile, 0)
        pair_copy(m, u).start()
        if u == 2 and m + 1 < batches:
            for s in range(1, ep_count):
                dispatch(m + 1, s).start()

    def add_pair(m, u):
        k = m * UNITS + u
        pair_copy(m, u).wait_recv()
        mine = rows_at(u * unit + low * half + (1 - high) * quarter, quarter)
        theirs = rows_at((1 - high) * quarter, quarter)

        def tile(i, carry):
            total = parts[m, mine, columns(i)].astype(jnp.float32) + pair_in[k, theirs, columns(i)].astype(jnp.float32)
            pair_in[k, theirs, columns(i)] = total.astype(jnp.bfloat16)
            return carry

        lax.fori_loop(0, 2 * units // TILE, tile, 0)
        cross_copy(m, u).start()

    def activate(m, u):
        k = m * UNITS + u
        cross_copy(m, u).wait_recv()
        mine = rows_at(u * unit + low * half + high * quarter, quarter)
        theirs = rows_at(high * quarter, quarter)

        def total(cols):
            return (
                parts[m, mine, cols].astype(jnp.float32)
                + pair_in[k, theirs, cols].astype(jnp.float32)
                + cross_in[k, :, cols].astype(jnp.float32)
            )

        def tile(i, carry):
            gate = total(columns(i))
            up = total(pl.ds(pl.multiple_of(units + i * TILE, TILE), TILE))
            hid[m, mine, columns(i)] = (jax.nn.silu(gate) * up).astype(jnp.bfloat16)
            return carry

        lax.fori_loop(0, units // TILE, tile, 0)
        hop_copy(m, u).start()

    def forward(m, u):
        hop_copy(m, u).wait_recv()
        fill_copy(m, u).start()

    def finish(m, u):
        fill_copy(m, u).wait_recv()
        if m == 0 and u == 0:
            weights[2].wait()
        rows = pl.ds(u * unit, unit)

        def tile(i, carry):
            eo[m, rows, columns(i)] = dot32(hid[m, rows, :], w_out[:, columns(i)]).astype(jnp.bfloat16)
            return carry

        lax.fori_loop(0, w_out.shape[1] // TILE, tile, 0)
        for s in range(u * per_unit, (u + 1) * per_unit):
            if s == 0:
                own_back(m).start()
            else:
                give_back(m, s).start()

    steps = [(m, u) for m in range(batches) for u in range(UNITS)]
    stages = (project, add_pair, activate, forward, finish)
    for step in range(len(steps) + len(stages) - 1):
        for lag, stage in enumerate(stages):
            if 0 <= step - lag < len(steps):
                stage(*steps[step - lag])

    for m in range(batches):
        combine(m)
    for m, u in steps:
        pair_copy(m, u).wait_send()
        cross_copy(m, u).wait_send()
        hop_copy(m, u).wait_send()
        fill_copy(m, u).wait_send()
    for m in range(batches):
        for s in range(1, ep_count):
            dispatch(m, s).wait_send()
            give_back(m, s).wait_send()
        own_row_back(m).wait()
        for p in range(len(peers)):
            slice_out(m, p).wait_send()
            row_back(m, p).wait_send()
            remote(
                rows_in.at[m, rows_at(peers[p] * tok_rows, tok_rows)],
                mixed.at[m, :, feats_at(peers[p])],
                out_send.at[m, p],
                out_recv.at[m, p],
                {"dp": peers[p]},
            ).wait_recv()


def run_experts(tokens, pick, factor, gain, table, gate, up, down, ep_count):
    batches, slots, group_rows = pick.shape
    feat = down.shape[1]
    units = gate.shape[1]
    count = batches * UNITS
    unit = slots // UNITS
    half, quarter = unit // 2, unit // 4
    bf16 = jnp.bfloat16
    dma = pltpu.SemaphoreType.DMA
    return pl.pallas_call(
        functools.partial(experts_kernel, ep_count, batches),
        out_shape=jax.ShapeDtypeStruct(tokens.shape, bf16),
        in_specs=[pl.BlockSpec(memory_space=pl.ANY)]
        + [pl.BlockSpec(memory_space=pltpu.VMEM)] * 4
        + [pl.BlockSpec(memory_space=pl.ANY)] * 3,
        out_specs=pl.BlockSpec(memory_space=pl.ANY),
        scratch_shapes=[
            pltpu.VMEM((feat, 2 * units), bf16),
            pltpu.VMEM((units, feat), bf16),
            pltpu.VMEM((batches, group_rows, feat), bf16),
            pltpu.VMEM((batches, slots, feat), bf16),
            pltpu.VMEM((batches, slots, feat), bf16),
            pltpu.VMEM((batches, group_rows, slots), bf16),
            pltpu.VMEM((batches, group_rows, slots), bf16),
            pltpu.VMEM((batches, group_rows, group_rows), bf16),
            pltpu.VMEM((batches, slots, feat), bf16),
            pltpu.VMEM((batches, slots, 2 * units), bf16),
            pltpu.VMEM((count, half, 2 * units), bf16),
            pltpu.VMEM((count, quarter, 2 * units), bf16),
            pltpu.VMEM((batches, slots, units), bf16),
            pltpu.VMEM((batches, slots, feat), bf16),
            dma((3,)),
            dma((2 * batches,)),
            dma((batches, ep_count)),
            dma((batches, ep_count)),
            dma((count,)),
            dma((count,)),
            dma((count,)),
            dma((count,)),
            dma((count,)),
            dma((count,)),
            dma((count,)),
            dma((count,)),
            dma((batches, ep_count)),
            dma((batches, ep_count)),
            dma((batches, 3)),
            dma((batches, 3)),
            dma((batches, 3)),
            dma((batches, 3)),
            dma((2 * batches,)),
        ],
        compiler_params=pltpu.CompilerParams(
            collective_id=0, has_side_effects=True, vmem_limit_bytes=60 * 1024 * 1024
        ),
        cost_estimate=pl.CostEstimate(
            flops=6 * batches * slots * feat * units, bytes_accessed=20 * 2**20, transcendentals=batches * slots * units
        ),
    )(tokens, pick, factor, gain, table, gate, up, down)


def local(hidden_in, norm_gain, span_plan, route_ids, route_gates, w_gate, w_up, w_down):
    dp_count = lax.axis_size("dp")
    ep_count = lax.axis_size("ep")
    dp_rank = lax.axis_index("dp")
    batches, tok_rows, width = hidden_in.shape
    routes = route_ids.shape[2]
    span_rows = tok_rows // SPANS
    group_rows = dp_count * tok_rows
    feat = width // dp_count
    capacity = -(-3 * group_rows * routes // (2 * ep_count) // 16) * 16
    slot_count = ep_count * capacity

    wide = hidden_in.astype(jnp.float32)
    factor = lax.rsqrt(jnp.mean(wide * wide, -1, keepdims=True) + 1e-06)
    facts = jnp.concatenate([factor, route_ids.astype(jnp.float32), route_gates], -1)
    facts = lax.all_gather(facts, "dp", axis=1, tiled=True)
    ids = facts[:, :, 1 : 1 + routes, None]
    gates = facts[:, :, 1 + routes :, None]
    gain = lax.dynamic_slice_in_dim(norm_gain, dp_rank * feat, feat, 0).astype(jnp.float32)

    experts = jnp.arange(ep_count, dtype=jnp.float32)
    slot_place = jnp.arange(capacity, dtype=jnp.float32)
    chosen = ids == experts
    named = jnp.sum(chosen.astype(jnp.float32), 2)
    numbers = jnp.arange(group_rows)
    earlier = (numbers[:, None] > numbers[None, :]).astype(jnp.bfloat16)
    place = jnp.einsum("ts,mse->mte", earlier, named.astype(jnp.bfloat16), preferred_element_type=jnp.float32)
    where = jnp.where(named > 0, place, -1.0)
    pick = (where.transpose(0, 2, 1)[:, :, None, :] == slot_place[None, None, :, None]).astype(jnp.bfloat16)
    pick = pick.reshape(batches, slot_count, group_rows)
    plan = span_plan[:, 0]
    slot = jnp.sum(jnp.where(chosen, experts * capacity + place[:, :, None, :], 0.0), -1)
    column = jnp.broadcast_to(numbers.astype(jnp.float32)[None, :, None], (batches, group_rows, 1))
    table = jnp.concatenate([slot, gates[..., 0], column], 2)
    table = table.reshape(batches, -1, span_rows, 2 * routes + 1)
    table = jnp.take_along_axis(table, plan[:, :, None, None], axis=1).reshape(batches, group_rows, -1)

    return run_experts(
        hidden_in,
        pick,
        facts[:, :, :1],
        gain[None, :],
        table,
        w_gate[0],
        w_up[0],
        w_down[0],
        ep_count,
    )


def solution(mesh):
    return jax.shard_map(
        local,
        mesh=mesh,
        in_specs=(
            P(None, ("grp", "ep", "dp"), None),
            P(),
            P(None, ("grp", "ep"), None),
            P(None, ("grp", "ep", "dp"), None),
            P(None, ("grp", "ep", "dp"), None),
            P("ep", "dp", None),
            P("ep", "dp", None),
            P("ep", None, "dp"),
        ),
        out_specs=P(None, ("grp", "ep", "dp"), None),
        check_vma=False,
    )
```
